32 devices in a mesh: tm: 8 (over z, y), panel: 4 (over x, core).
Axes of the slice: x: 2, y: 2, z: 4, core: 2. Of those that a mesh axis runs over, the one named last changes fastest.
Arguments:
- transitions: float32 [16, 1024, 1024], P('tm', None, 'panel'), may hold values from 0 to 1, as said below
- start_weights: float32 [1024], replicated, may hold values from 0.1 to 10
Outputs:
- window_kernel: float32 [8, 1024, 1024], P('tm', None, 'panel')
- occupancy: float32 [8, 1024], P('tm', 'panel')
The draws below stay inside these ranges and needn't reach their ends.
Inputs may be any that keep to these rules, and one draw needn't show every extreme that they name: `transitions`: every entry is nonnegative; each diagonal entry is 0.3 or more; each row sums to between 0.3 and 1.7.
All inputs are finite; a program needn't handle non-finite values.
Results may differ from the reference program's by a relative error of at most 0.0003.
Values sent between devices are 32-bit elements; how exact they have to be, the bound alone decides.
A program may use at most 64 MiB of HBM per device.

```python
import math
import jax
import jax.numpy as jnp
from jax import lax

S = 1024
BLOCK = 2
LEVELS = 2
STEPS = 16
N_TM = 8


def draw_transitions(key, part):
    key_stay = jax.random.fold_in(key, 11)
    key_move = jax.random.fold_in(key, 12)
    stay = jax.random.uniform(key_stay, (STEPS, S, 1), jnp.float32, 0.3, 0.9)
    spread = jax.random.uniform(key_move, (STEPS, S, S), jnp.float32, 0.0, 1.0)
    rows_index = jnp.arange(S)[:, None]
    cols_index = jnp.arange(S)[None, :]
    identity = (rows_index == cols_index).astype(jnp.float32)
    half_width = max(2, min(32, S // 16))
    offset = (cols_index - rows_index - S // 4) % S
    distance = jnp.minimum(offset, S - offset)
    band = (distance <= half_width).astype(jnp.float32)
    weights = 0.5 / S + band * (1.5 / (2 * half_width + 1))
    return (1.0 - stay) * spread * weights + stay * identity


def setup_inputs(seed: int = 0) -> dict:
    seeds = jax.random.split(jax.random.key(seed), 3)
    return {
        "transitions": draw_transitions(jax.random.fold_in(seeds[2], 71), 0),
        "start_weights": jnp.clip(jnp.exp(jax.random.uniform(seeds[1], (S,), jnp.float32, math.log(0.1), math.log(10.0))), 0.1, 10.0),
    }


def matmul_high(left, right):
    return jnp.matmul(left, right, precision=lax.Precision.HIGHEST)


def reference(transitions, start_weights):
    blocks = transitions.reshape(N_TM, BLOCK, S, S)
    running = blocks[:, 0]
    for step in range(1, BLOCK):
        running = matmul_high(running, blocks[:, step])
    for level in range(LEVELS):
        reach = 2 ** level
        joined = matmul_high(running[:-reach], running[reach:])
        running = jnp.concatenate([running[:reach], joined], axis=0)
    window_kernel = running * jnp.float32(S)
    occupancy = jnp.einsum("s,bst->bt", start_weights, running, precision=lax.Precision.HIGHEST)
    return window_kernel, occupancy
```

```python
import functools

import jax
import jax.numpy as jnp
from jax import lax
from jax.experimental import pallas as pl
from jax.experimental.pallas import tpu as pltpu
from jax.sharding import PartitionSpec as P

LEVELS = 2
CHUNKS = 8
MESH = pl.DeviceIdType.MESH
HI = jnp.bfloat16


def split(value):
    high = value.astype(HI)
    return high, (value - high.astype(jnp.float32)).astype(HI)


def kernel(n_tm, n_panel, steps_ref, weights_ref, window_ref, occ_ref,
           full, right_f32, right_hi, right_lo,
           lo_send, lo_recv, hi_send, hi_recv, rel_send, rel_recv, tm_send, tm_recv):
    states, width = steps_ref.shape[1:]
    rows = states // CHUNKS
    halves = n_panel // 2
    t = lax.axis_index("tm")
    p = lax.axis_index("panel")
    hi, lo = p // 2, p % 2
    partner = hi * 2 + (1 - lo)

    def other(k):
        return lax.rem(hi + k, halves) * 2 + lo

    def back(k):
        return lax.rem(hi + halves - k, halves) * 2 + lo

    barrier = pltpu.get_barrier_semaphore()
    pl.semaphore_signal(barrier, inc=1, device_id={"panel": partner}, device_id_type=MESH)
    for k in range(1, halves):
        pl.semaphore_signal(barrier, inc=1, device_id={"panel": other(k)}, device_id_type=MESH)
    reaches = [2**level for level in range(LEVELS)]
    for reach in reaches:
        @pl.when(t + reach < n_tm)
        def _():
            pl.semaphore_signal(barrier, inc=1, device_id={"tm": t + reach}, device_id_type=MESH)

        @pl.when(t >= reach)
        def _():
            pl.semaphore_signal(barrier, inc=1, device_id={"tm": t - reach}, device_id_type=MESH)
    peers = halves
    for reach in reaches:
        peers += (t + reach < n_tm).astype(jnp.int32) + (t >= reach).astype(jnp.int32)
    pl.semaphore_wait(barrier, peers)

    def band(r):
        return pl.ds(pl.multiple_of(r * rows, rows), rows)

    def own(stage, r):
        return steps_ref.at[0, band(r)] if stage == 0 else full.at[stage, p, band(r)]

    def to_partner(stage, r):
        return pltpu.make_async_remote_copy(
            own(stage, r), full.at[stage, p, band(r)],
            lo_send.at[stage, r], lo_recv.at[stage, r],
            device_id={"panel": partner}, device_id_type=MESH)

    def to_other(stage, r, k):
        return pltpu.make_async_remote_copy(
            own(stage, r), full.at[stage, p, band(r)],
            hi_send.at[stage, k - 1, r], hi_recv.at[stage, k - 1, r],
            device_id={"panel": other(k)}, device_id_type=MESH)

    def relayed(stage, r, k):
        slot = full.at[stage, back(k), band(r)]
        return pltpu.make_async_remote_copy(
            slot, slot, rel_send.at[stage, k - 1, r], rel_recv.at[stage, k - 1, r],
            device_id={"panel": partner}, device_id_type=MESH)

    def along(stage, r):
        reach = reaches[stage]
        return pltpu.make_async_remote_copy(
            right_f32.at[stage, band(r)], full.at[stage + 1, p, band(r)],
            tm_send.at[stage, r], tm_recv.at[stage, r],
            device_id={"tm": t + reach}, device_id_type=MESH)

    def forward(stage, r):
        if stage:
            along(stage - 1, r).wait_recv()
        for k in range(1, halves):
            to_other(stage, r, k).start()
        to_partner(stage, r).start()

    def relay(stage, r):
        for k in range(1, halves):
            to_other(stage, r, k).wait_recv()
            relayed(stage, r, k).start()

    def product(stage, r):
        to_partner(stage, r).wait_recv()
        for k in range(1, halves):
            relayed(stage, r, k).wait_recv()
        total = jnp.zeros((rows, width), jnp.float32)
        for k in range(n_panel):
            a_hi, a_lo = split(full[stage, k, band(r), :])
            cols = pl.ds(k * width, width)
            b_hi, b_lo = right_hi[stage, cols, :], right_lo[stage, cols, :]
            both = jnp.dot(jnp.concatenate([a_hi, a_lo], axis=0), b_hi,
                           preferred_element_type=jnp.float32)
            total += both[:rows] + both[rows:] + jnp.dot(
                a_hi, b_lo, preferred_element_type=jnp.float32)
        return total

    def put(stage, r, value):
        if stage < LEVELS:
            right_f32[stage, band(r), :] = value
            high, low = split(value)
            right_hi[stage + 1, band(r), :] = high
            right_lo[stage + 1, band(r), :] = low

            @pl.when(t + reaches[stage] < n_tm)
            def _():
                along(stage, r).start()
        else:
            window_ref[band(r), :] = value
            line = jnp.broadcast_to(weights_ref[pl.ds(r, 1), :], (8, rows))
            occ_ref[...] += jnp.dot(line, value, precision=lax.Precision.HIGHEST,
                                    preferred_element_type=jnp.float32)

    def compute(stage, r):
        if stage == 0:
            full[0, p, band(r), :] = steps_ref[0, band(r), :]
            put(0, r, product(0, r))
        else:
            reach = reaches[stage - 1]

            @pl.when(t >= reach)
            def _():
                put(stage, r, product(stage, r))

            @pl.when(t < reach)
            def _():
                put(stage, r, right_f32[stage - 1, band(r), :])

    def first(r, carry):
        forward(0, r)
        return carry

    lax.fori_loop(0, CHUNKS, first, 0)
    occ_ref[...] = jnp.zeros_like(occ_ref)

    def prepare(r, carry):
        high, low = split(steps_ref[1, band(r), :])
        right_hi[0, band(r), :] = high
        right_lo[0, band(r), :] = low
        return carry

    lax.fori_loop(0, CHUNKS, prepare, 0)

    relay_at = [0, CHUNKS + 1, 2 * CHUNKS + 2]
    forward_at = [None, 3, CHUNKS + 4]

    def step(s, carry):
        def at(begin, do, needs):
            r = s - begin

            @pl.when(jnp.logical_and(jnp.logical_and(r >= 0, r < CHUNKS), needs))
            def _():
                do(r)

        for stage in range(LEVELS + 1):
            needs = t >= (reaches[stage - 1] if stage else 0)
            at(relay_at[stage], functools.partial(relay, stage), needs)
        for stage in range(1, LEVELS + 1):
            at(forward_at[stage], functools.partial(forward, stage), t >= reaches[stage - 1])
        for stage in range(LEVELS + 1):
            at(relay_at[stage] + 1, functools.partial(compute, stage), t >= 0)
        return carry

    lax.fori_loop(0, 3 * CHUNKS + 3, step, 0)

    def drain(r, carry):
        for stage in range(LEVELS + 1):
            @pl.when(t >= (reaches[stage - 1] if stage else 0))
            def _():
                to_partner(stage, r).wait_send()
                for k in range(1, halves):
                    to_other(stage, r, k).wait_send()
                    relayed(stage, r, k).wait_send()
        for stage in range(LEVELS):
            @pl.when(t + reaches[stage] < n_tm)
            def _():
                along(stage, r).wait_send()
        return carry

    lax.fori_loop(0, CHUNKS, drain, 0)


def body(transitions, start_weights):
    _, states, width = transitions.shape
    n_tm, n_panel = lax.axis_size("tm"), lax.axis_size("panel")
    others = n_panel // 2 - 1
    stages = LEVELS + 1
    dma = pltpu.SemaphoreType.DMA
    size = states * width * 4
    window, occupancy = pl.pallas_call(
        functools.partial(kernel, n_tm, n_panel),
        out_shape=(jax.ShapeDtypeStruct((states, width), jnp.float32),
                   jax.ShapeDtypeStruct((8, width), jnp.float32)),
        in_specs=[pl.BlockSpec(memory_space=pltpu.VMEM)] * 2,
        out_specs=[pl.BlockSpec(memory_space=pltpu.VMEM)] * 2,
        scratch_shapes=[
            pltpu.VMEM((stages, n_panel, states, width), jnp.float32),
            pltpu.VMEM((LEVELS, states, width), jnp.float32),
            pltpu.VMEM((stages, states, width), jnp.bfloat16),
            pltpu.VMEM((stages, states, width), jnp.bfloat16),
            dma((stages, CHUNKS)), dma((stages, CHUNKS)),
            dma((stages, others, CHUNKS)), dma((stages, others, CHUNKS)),
            dma((stages, others, CHUNKS)), dma((stages, others, CHUNKS)),
            dma((LEVELS, CHUNKS)), dma((LEVELS, CHUNKS)),
        ],
        compiler_params=pltpu.CompilerParams(
            collective_id=0, has_side_effects=True,
            vmem_limit_bytes=size * (stages * n_panel + 3 * stages + 8)),
    )(transitions, start_weights.reshape(CHUNKS, states // CHUNKS))
    window_kernel = (window * jnp.float32(states))[None]
    return (window_kernel, occupancy[:1])


def solution(mesh):
    placed = (P("tm", None, "panel"), P())
    return jax.shard_map(
        body,
        mesh=mesh,
        in_specs=placed,
        out_specs=(P("tm", None, "panel"), P("tm", "panel")),
        check_vma=False,
    )
```

```python
import functools

import jax
import jax.numpy as jnp
from jax import lax
from jax.experimental import pallas as pl
from jax.experimental.pallas import tpu as pltpu
from jax.sharding import PartitionSpec as P

LEVELS = 2
CHUNKS = 16
MESH = pl.DeviceIdType.MESH
HI = jnp.bfloat16


def split(value):
    high = value.astype(HI)
    return high, (value - high.astype(jnp.float32)).astype(HI)


def kernel(n_tm, n_panel, steps_ref, weights_ref, window_ref, occ_ref,
           full, last, right_f32, right_hi, right_lo, fetch,
           lo_send, lo_recv, hi_send, hi_recv, rel_send, rel_recv, tm_send, tm_recv):
    states, width = steps_ref.shape[1:]
    rows = states // CHUNKS
    halves = n_panel // 2
    t = lax.axis_index("tm")
    p = lax.axis_index("panel")
    hi, lo = p // 2, p % 2
    partner = hi * 2 + (1 - lo)

    def other(k):
        return lax.rem(hi + k, halves) * 2 + lo

    def back(k):
        return lax.rem(hi + halves - k, halves) * 2 + lo

    first_in = pltpu.make_async_copy(steps_ref.at[0], full.at[0, p], fetch.at[0])
    last_in = pltpu.make_async_copy(steps_ref.at[1], last, fetch.at[1])
    last_in.start()
    first_in.start()

    barrier = pltpu.get_barrier_semaphore()
    pl.semaphore_signal(barrier, inc=1, device_id={"panel": partner}, device_id_type=MESH)
    for k in range(1, halves):
        pl.semaphore_signal(barrier, inc=1, device_id={"panel": other(k)}, device_id_type=MESH)
    reaches = [2**level for level in range(LEVELS)]
    for reach in reaches:
        @pl.when(t + reach < n_tm)
        def _():
            pl.semaphore_signal(barrier, inc=1, device_id={"tm": t + reach}, device_id_type=MESH)

        @pl.when(t >= reach)
        def _():
            pl.semaphore_signal(barrier, inc=1, device_id={"tm": t - reach}, device_id_type=MESH)
    peers = halves
    for reach in reaches:
        peers += (t + reach < n_tm).astype(jnp.int32) + (t >= reach).astype(jnp.int32)
    pl.semaphore_wait(barrier, peers)

    def band(r):
        return pl.ds(pl.multiple_of(r * rows, rows), rows)

    def own(stage, r):
        return steps_ref.at[0, band(r)] if stage == 0 else full.at[stage, p, band(r)]

    def to_partner(stage, r):
        return pltpu.make_async_remote_copy(
            own(stage, r), full.at[stage, p, band(r)],
            lo_send.at[stage, r], lo_recv.at[stage, r],
            device_id={"panel": partner}, device_id_type=MESH)

    def to_other(stage, r, k):
        return pltpu.make_async_remote_copy(
            own(stage, r), full.at[stage, p, band(r)],
            hi_send.at[stage, k - 1, r], hi_recv.at[stage, k - 1, r],
            device_id={"panel": other(k)}, device_id_type=MESH)

    def relayed(stage, r, k):
        slot = full.at[stage, back(k), band(r)]
        return pltpu.make_async_remote_copy(
            slot, slot, rel_send.at[stage, k - 1, r], rel_recv.at[stage, k - 1, r],
            device_id={"panel": partner}, device_id_type=MESH)

    def along(stage, r):
        reach = reaches[stage]
        return pltpu.make_async_remote_copy(
            right_f32.at[stage, band(r)], full.at[stage + 1, p, band(r)],
            tm_send.at[stage, r], tm_recv.at[stage, r],
            device_id={"tm": t + reach}, device_id_type=MESH)

    def forward(stage, r):
        if stage:
            along(stage - 1, r).wait_recv()
        for k in range(1, halves):
            to_other(stage, r, k).start()
        to_partner(stage, r).start()

    def relay(stage, r):
        for k in range(1, halves):
            to_other(stage, r, k).wait_recv()
            relayed(stage, r, k).start()

    def product(stage, r):
        to_partner(stage, r).wait_recv()
        for k in range(1, halves):
            relayed(stage, r, k).wait_recv()
        total = jnp.zeros((rows, width), jnp.float32)
        for k in range(n_panel):
            a_hi, a_lo = split(full[stage, k, band(r), :])
            cols = pl.ds(k * width, width)
            b_hi, b_lo = right_hi[stage, cols, :], right_lo[stage, cols, :]
            both = jnp.dot(jnp.concatenate([a_hi, a_lo], axis=0), b_hi,
                           preferred_element_type=jnp.float32)
            total += both[:rows] + both[rows:] + jnp.dot(
                a_hi, b_lo, preferred_element_type=jnp.float32)
        return total

    def put(stage, r, value):
        if stage < LEVELS:
            right_f32[stage, band(r), :] = value
            high, low = split(value)
            right_hi[stage + 1, band(r), :] = high
            right_lo[stage + 1, band(r), :] = low

            @pl.when(t + reaches[stage] < n_tm)
            def _():
                along(stage, r).start()
        else:
            window_ref[band(r), :] = value
            line = jnp.broadcast_to(weights_ref[pl.ds(r, 1), :], (8, rows))
            occ_ref[...] += jnp.dot(line, value, precision=lax.Precision.HIGHEST,
                                    preferred_element_type=jnp.float32)[:1]

    def compute(stage, r):
        if stage == 0:
            put(0, r, product(0, r))
        else:
            reach = reaches[stage - 1]

            @pl.when(t >= reach)
            def _():
                put(stage, r, product(stage, r))

            @pl.when(t < reach)
            def _():
                put(stage, r, right_f32[stage - 1, band(r), :])

    def first(r, carry):
        forward(0, r)
        return carry

    lax.fori_loop(0, CHUNKS, first, 0)
    occ_ref[...] = jnp.zeros_like(occ_ref)
    last_in.wait()

    def prepare(r, carry):
        high, low = split(last[band(r), :])
        right_hi[0, band(r), :] = high
        right_lo[0, band(r), :] = low
        return carry

    lax.fori_loop(0, CHUNKS, prepare, 0)
    first_in.wait()

    relay_at = [0, CHUNKS + 1, 2 * CHUNKS + 2]
    forward_at = [None, 3, CHUNKS + 4]

    def step(s, carry):
        def at(begin, do, needs):
            r = s - begin

            @pl.when(jnp.logical_and(jnp.logical_and(r >= 0, r < CHUNKS), needs))
            def _():
                do(r)

        for stage in range(LEVELS + 1):
            needs = t >= (reaches[stage - 1] if stage else 0)
            at(relay_at[stage], functools.partial(relay, stage), needs)
        for stage in range(1, LEVELS + 1):
            at(forward_at[stage], functools.partial(forward, stage), t >= reaches[stage - 1])
        for stage in range(LEVELS + 1):
            at(relay_at[stage] + 1, functools.partial(compute, stage), t >= 0)
        return carry

    lax.fori_loop(0, 3 * CHUNKS + 3, step, 0)

    def drain(r, carry):
        for stage in range(LEVELS + 1):
            @pl.when(t >= (reaches[stage - 1] if stage else 0))
            def _():
                to_partner(stage, r).wait_send()
                for k in range(1, halves):
                    to_other(stage, r, k).wait_send()
                    relayed(stage, r, k).wait_send()
        for stage in range(LEVELS):
            @pl.when(t + reaches[stage] < n_tm)
            def _():
                along(stage, r).wait_send()
        return carry

    lax.fori_loop(0, CHUNKS, drain, 0)


def body(transitions, start_weights):
    _, states, width = transitions.shape
    n_tm, n_panel = lax.axis_size("tm"), lax.axis_size("panel")
    others = n_panel // 2 - 1
    stages = LEVELS + 1
    dma = pltpu.SemaphoreType.DMA
    size = states * width * 4
    window, occupancy = pl.pallas_call(
        functools.partial(kernel, n_tm, n_panel),
        out_shape=(jax.ShapeDtypeStruct((states, width), jnp.float32),
                   jax.ShapeDtypeStruct((1, width), jnp.float32)),
        in_specs=[pl.BlockSpec(memory_space=pltpu.HBM), pl.BlockSpec(memory_space=pltpu.VMEM)],
        out_specs=[pl.BlockSpec(memory_space=pltpu.VMEM)] * 2,
        scratch_shapes=[
            pltpu.VMEM((stages, n_panel, states, width), jnp.float32),
            pltpu.VMEM((states, width), jnp.float32),
            pltpu.VMEM((LEVELS, states, width), jnp.float32),
            pltpu.VMEM((stages, states, width), jnp.bfloat16),
            pltpu.VMEM((stages, states, width), jnp.bfloat16),
            dma((2,)),
            dma((stages, CHUNKS)), dma((stages, CHUNKS)),
            dma((stages, others, CHUNKS)), dma((stages, others, CHUNKS)),
            dma((stages, others, CHUNKS)), dma((stages, others, CHUNKS)),
            dma((LEVELS, CHUNKS)), dma((LEVELS, CHUNKS)),
        ],
        compiler_params=pltpu.CompilerParams(
            collective_id=0, has_side_effects=True,
            vmem_limit_bytes=size * (stages * n_panel + 3 * stages + 8)),
    )(transitions, start_weights.reshape(CHUNKS, states // CHUNKS))
    window_kernel = (window * jnp.float32(states))[None]
    return (window_kernel, occupancy)


def solution(mesh):
    placed = (P("tm", None, "panel"), P())
    return jax.shard_map(
        body,
        mesh=mesh,
        in_specs=placed,
        out_specs=(P("tm", None, "panel"), P("tm", "panel")),
        check_vma=False,
    )
```

```python
import functools

import jax
import jax.numpy as jnp
from jax import lax
from jax.experimental import pallas as pl
from jax.experimental.pallas import tpu as pltpu
from jax.sharding import PartitionSpec as P

LEVELS = 2
CHUNKS = 8
MESH = pl.DeviceIdType.MESH
HI = jnp.bfloat16


def split(value):
    high = value.astype(HI)
    return high, (value - high.astype(jnp.float32)).astype(HI)


def kernel(n_tm, n_panel, steps_ref, weights_ref, window_ref, occ_ref,
           full, right_f32, right_hi, right_lo,
           lo_send, lo_recv, hi_send, hi_recv, rel_send, rel_recv, tm_send, tm_recv):
    states, width = steps_ref.shape[1:]
    rows = states // CHUNKS
    halves = n_panel // 2
    t = lax.axis_index("tm")
    p = lax.axis_index("panel")
    hi, lo = p // 2, p % 2
    partner = hi * 2 + (1 - lo)

    def other(k):
        return lax.rem(hi + k, halves) * 2 + lo

    def back(k):
        return lax.rem(hi + halves - k, halves) * 2 + lo

    barrier = pltpu.get_barrier_semaphore()
    pl.semaphore_signal(barrier, inc=1, device_id={"panel": partner}, device_id_type=MESH)
    for k in range(1, halves):
        pl.semaphore_signal(barrier, inc=1, device_id={"panel": other(k)}, device_id_type=MESH)
    reaches = [2**level for level in range(LEVELS)]
    for reach in reaches:
        @pl.when(t + reach < n_tm)
        def _():
            pl.semaphore_signal(barrier, inc=1, device_id={"tm": t + reach}, device_id_type=MESH)

        @pl.when(t >= reach)
        def _():
            pl.semaphore_signal(barrier, inc=1, device_id={"tm": t - reach}, device_id_type=MESH)
    peers = halves
    for reach in reaches:
        peers += (t + reach < n_tm).astype(jnp.int32) + (t >= reach).astype(jnp.int32)
    pl.semaphore_wait(barrier, peers)

    def band(r):
        return pl.ds(pl.multiple_of(r * rows, rows), rows)

    def own(stage, r):
        return steps_ref.at[0, band(r)] if stage == 0 else full.at[stage, p, band(r)]

    def to_partner(stage, r):
        return pltpu.make_async_remote_copy(
            own(stage, r), full.at[stage, p, band(r)],
            lo_send.at[stage, r], lo_recv.at[stage, r],
            device_id={"panel": partner}, device_id_type=MESH)

    def to_other(stage, r, k):
        return pltpu.make_async_remote_copy(
            own(stage, r), full.at[stage, p, band(r)],
            hi_send.at[stage, k - 1, r], hi_recv.at[stage, k - 1, r],
            device_id={"panel": other(k)}, device_id_type=MESH)

    def relayed(stage, r, k):
        slot = full.at[stage, back(k), band(r)]
        return pltpu.make_async_remote_copy(
            slot, slot, rel_send.at[stage, k - 1, r], rel_recv.at[stage, k - 1, r],
            device_id={"panel": partner}, device_id_type=MESH)

    def along(stage, r):
        reach = reaches[stage]
        return pltpu.make_async_remote_copy(
            right_f32.at[stage, band(r)], full.at[stage + 1, p, band(r)],
            tm_send.at[stage, r], tm_recv.at[stage, r],
            device_id={"tm": t + reach}, device_id_type=MESH)

    def forward(stage, r):
        if stage:
            along(stage - 1, r).wait_recv()
        for k in range(1, halves):
            to_other(stage, r, k).start()
        to_partner(stage, r).start()

    def relay(stage, r):
        for k in range(1, halves):
            to_other(stage, r, k).wait_recv()
            relayed(stage, r, k).start()

    def product(stage, r):
        to_partner(stage, r).wait_recv()
        for k in range(1, halves):
            relayed(stage, r, k).wait_recv()
        total = jnp.zeros((rows, width), jnp.float32)
        for k in range(n_panel):
            a_hi, a_lo = split(full[stage, k, band(r), :])
            cols = pl.ds(k * width, width)
            b_hi, b_lo = right_hi[stage, cols, :], right_lo[stage, cols, :]
            both = jnp.dot(jnp.concatenate([a_hi, a_lo], axis=0), b_hi,
                           preferred_element_type=jnp.float32)
            total += both[:rows] + both[rows:] + jnp.dot(
                a_hi, b_lo, preferred_element_type=jnp.float32)
        return total

    def put(stage, r, value):
        if stage < LEVELS:
            right_f32[stage, band(r), :] = value
            high, low = split(value)
            right_hi[stage + 1, band(r), :] = high
            right_lo[stage + 1, band(r), :] = low

            @pl.when(t + reaches[stage] < n_tm)
            def _():
                along(stage, r).start()
        else:
            window_ref[band(r), :] = value * jnp.float32(states)
            line = jnp.broadcast_to(weights_ref[pl.ds(r, 1), :], (8, rows))
            occ_ref[...] += jnp.dot(line, value, precision=lax.Precision.HIGHEST,
                                    preferred_element_type=jnp.float32)

    def compute(stage, r):
        if stage == 0:
            full[0, p, band(r), :] = steps_ref[0, band(r), :]
            put(0, r, product(0, r))
        else:
            reach = reaches[stage - 1]

            @pl.when(t >= reach)
            def _():
                put(stage, r, product(stage, r))

            @pl.when(t < reach)
            def _():
                put(stage, r, right_f32[stage - 1, band(r), :])

    def first(r, carry):
        forward(0, r)
        return carry

    lax.fori_loop(0, CHUNKS, first, 0)
    occ_ref[...] = jnp.zeros_like(occ_ref)

    def prepare(r, carry):
        high, low = split(steps_ref[1, band(r), :])
        right_hi[0, band(r), :] = high
        right_lo[0, band(r), :] = low
        return carry

    lax.fori_loop(0, CHUNKS, prepare, 0)

    relay_at = [0, CHUNKS + 1, 2 * CHUNKS + 2]
    forward_at = [None, 3, CHUNKS + 4]

    def step(s, carry):
        def at(begin, do, needs):
            r = s - begin

            @pl.when(jnp.logical_and(jnp.logical_and(r >= 0, r < CHUNKS), needs))
            def _():
                do(r)

        for stage in range(LEVELS + 1):
            needs = t >= (reaches[stage - 1] if stage else 0)
            at(relay_at[stage], functools.partial(relay, stage), needs)
        for stage in range(1, LEVELS + 1):
            at(forward_at[stage], functools.partial(forward, stage), t >= reaches[stage - 1])
        for stage in range(LEVELS + 1):
            at(relay_at[stage] + 1, functools.partial(compute, stage), t >= 0)
        return carry

    lax.fori_loop(0, 3 * CHUNKS + 3, step, 0)

    def drain(r, carry):
        for stage in range(LEVELS + 1):
            @pl.when(t >= (reaches[stage - 1] if stage else 0))
            def _():
                to_partner(stage, r).wait_send()
                for k in range(1, halves):
                    to_other(stage, r, k).wait_send()
                    relayed(stage, r, k).wait_send()
        for stage in range(LEVELS):
            @pl.when(t + reaches[stage] < n_tm)
            def _():
                along(stage, r).wait_send()
        return carry

    lax.fori_loop(0, CHUNKS, drain, 0)


def body(transitions, start_weights):
    _, states, width = transitions.shape
    n_tm, n_panel = lax.axis_size("tm"), lax.axis_size("panel")
    others = n_panel // 2 - 1
    stages = LEVELS + 1
    dma = pltpu.SemaphoreType.DMA
    size = states * width * 4
    window, occupancy = pl.pallas_call(
        functools.partial(kernel, n_tm, n_panel),
        out_shape=(jax.ShapeDtypeStruct((states, width), jnp.float32),
                   jax.ShapeDtypeStruct((8, width), jnp.float32)),
        in_specs=[pl.BlockSpec(memory_space=pltpu.VMEM)] * 2,
        out_specs=[pl.BlockSpec(memory_space=pltpu.VMEM)] * 2,
        scratch_shapes=[
            pltpu.VMEM((stages, n_panel, states, width), jnp.float32),
            pltpu.VMEM((LEVELS, states, width), jnp.float32),
            pltpu.VMEM((stages, states, width), jnp.bfloat16),
            pltpu.VMEM((stages, states, width), jnp.bfloat16),
            dma((stages, CHUNKS)), dma((stages, CHUNKS)),
            dma((stages, others, CHUNKS)), dma((stages, others, CHUNKS)),
            dma((stages, others, CHUNKS)), dma((stages, others, CHUNKS)),
            dma((LEVELS, CHUNKS)), dma((LEVELS, CHUNKS)),
        ],
        compiler_params=pltpu.CompilerParams(
            collective_id=0, has_side_effects=True,
            vmem_limit_bytes=size * (stages * n_panel + 3 * stages + 8)),
    )(transitions, start_weights.reshape(CHUNKS, states // CHUNKS))
    window_kernel = window[None]
    return (window_kernel, occupancy[:1])


def solution(mesh):
    placed = (P("tm", None, "panel"), P())
    return jax.shard_map(
        body,
        mesh=mesh,
        in_specs=placed,
        out_specs=(P("tm", None, "panel"), P("tm", "panel")),
        check_vma=False,
    )
```

```python
import functools

import jax
import jax.numpy as jnp
from jax import lax
from jax.experimental import pallas as pl
from jax.experimental.pallas import tpu as pltpu
from jax.sharding import PartitionSpec as P

LEVELS = 2
CHUNKS = 8
MESH = pl.DeviceIdType.MESH
HI = jnp.bfloat16


def split(value):
    high = value.astype(HI)
    return high, (value - high.astype(jnp.float32)).astype(HI)


def kernel(n_tm, n_panel, steps_ref, weights_ref, window_ref, occ_ref,
           full, right_f32, right_hi, right_lo,
           lo_send, lo_recv, hi_send, hi_recv, rel_send, rel_recv, tm_send, tm_recv):
    states, width = steps_ref.shape[1:]
    rows = states // CHUNKS
    halves = n_panel // 2
    t = lax.axis_index("tm")
    p = lax.axis_index("panel")
    hi, lo = p // 2, p % 2
    partner = hi * 2 + (1 - lo)

    def other(k):
        return lax.rem(hi + k, halves) * 2 + lo

    def back(k):
        return lax.rem(hi + halves - k, halves) * 2 + lo

    barrier = pltpu.get_barrier_semaphore()
    pl.semaphore_signal(barrier, inc=1, device_id={"panel": partner}, device_id_type=MESH)
    for k in range(1, halves):
        pl.semaphore_signal(barrier, inc=1, device_id={"panel": other(k)}, device_id_type=MESH)
    reaches = [2**level for level in range(LEVELS)]
    for reach in reaches:
        @pl.when(t + reach < n_tm)
        def _():
            pl.semaphore_signal(barrier, inc=1, device_id={"tm": t + reach}, device_id_type=MESH)

        @pl.when(t >= reach)
        def _():
            pl.semaphore_signal(barrier, inc=1, device_id={"tm": t - reach}, device_id_type=MESH)
    peers = halves
    for reach in reaches:
        peers += (t + reach < n_tm).astype(jnp.int32) + (t >= reach).astype(jnp.int32)
    pl.semaphore_wait(barrier, peers)

    def band(r):
        return pl.ds(pl.multiple_of(r * rows, rows), rows)

    def own(stage, r):
        return steps_ref.at[0, band(r)] if stage == 0 else full.at[stage, p, band(r)]

    def to_partner(stage, r):
        return pltpu.make_async_remote_copy(
            own(stage, r), full.at[stage, p, band(r)],
            lo_send.at[stage, r], lo_recv.at[stage, r],
            device_id={"panel": partner}, device_id_type=MESH)

    def to_other(stage, r, k):
        return pltpu.make_async_remote_copy(
            own(stage, r), full.at[stage, p, band(r)],
            hi_send.at[stage, k - 1, r], hi_recv.at[stage, k - 1, r],
            device_id={"panel": other(k)}, device_id_type=MESH)

    def relayed(stage, r, k):
        slot = full.at[stage, back(k), band(r)]
        return pltpu.make_async_remote_copy(
            slot, slot, rel_send.at[stage, k - 1, r], rel_recv.at[stage, k - 1, r],
            device_id={"panel": partner}, device_id_type=MESH)

    def along(stage, r):
        reach = reaches[stage]
        return pltpu.make_async_remote_copy(
            right_f32.at[stage, band(r)], full.at[stage + 1, p, band(r)],
            tm_send.at[stage, r], tm_recv.at[stage, r],
            device_id={"tm": t + reach}, device_id_type=MESH)

    def forward(stage, r):
        if stage:
            along(stage - 1, r).wait_recv()
        for k in range(1, halves):
            to_other(stage, r, k).start()
        to_partner(stage, r).start()

    def relay(stage, r):
        for k in range(1, halves):
            to_other(stage, r, k).wait_recv()
            relayed(stage, r, k).start()

    def product(stage, r):
        to_partner(stage, r).wait_recv()
        for k in range(1, halves):
            relayed(stage, r, k).wait_recv()
        total = jnp.zeros((rows, width), jnp.float32)
        for k in range(n_panel):
            a_hi, a_lo = split(full[stage, k, band(r), :])
            cols = pl.ds(k * width, width)
            b_hi, b_lo = right_hi[stage, cols, :], right_lo[stage, cols, :]
            both = jnp.dot(jnp.concatenate([a_hi, a_lo], axis=0), b_hi,
                           preferred_element_type=jnp.float32)
            total += both[:rows] + both[rows:] + jnp.dot(
                a_hi, b_lo, preferred_element_type=jnp.float32)
        return total

    def put(stage, r, value):
        if stage < LEVELS:
            right_f32[stage, band(r), :] = value
            high, low = split(value)
            right_hi[stage + 1, band(r), :] = high
            right_lo[stage + 1, band(r), :] = low

            @pl.when(t + reaches[stage] < n_tm)
            def _():
                along(stage, r).start()
        else:
            window_ref[band(r), :] = value * jnp.float32(states)
            line = jnp.broadcast_to(weights_ref[pl.ds(r, 1), :], (8, rows))
            occ_ref[...] += jnp.dot(line, value, precision=lax.Precision.HIGHEST,
                                    preferred_element_type=jnp.float32)[:1]

    def compute(stage, r):
        if stage == 0:
            full[0, p, band(r), :] = steps_ref[0, band(r), :]
            put(0, r, product(0, r))
        else:
            reach = reaches[stage - 1]

            @pl.when(t >= reach)
            def _():
                put(stage, r, product(stage, r))

            @pl.when(t < reach)
            def _():
                put(stage, r, right_f32[stage - 1, band(r), :])

    def first(r, carry):
        for k in range(1, halves):
            to_other(0, r, k).start()
        return carry

    def first_partner(r, carry):
        to_partner(0, r).start()
        return carry

    lax.fori_loop(0, CHUNKS, first, 0)
    lax.fori_loop(0, CHUNKS, first_partner, 0)
    occ_ref[...] = jnp.zeros_like(occ_ref)

    def prepare(r, carry):
        high, low = split(steps_ref[1, band(r), :])
        right_hi[0, band(r), :] = high
        right_lo[0, band(r), :] = low
        return carry

    lax.fori_loop(0, CHUNKS, prepare, 0)

    relay_at = [0, CHUNKS + 1, 2 * CHUNKS + 2]
    forward_at = [None, 3, CHUNKS + 4]

    def step(s, carry):
        def at(begin, do, needs):
            r = s - begin

            @pl.when(jnp.logical_and(jnp.logical_and(r >= 0, r < CHUNKS), needs))
            def _():
                do(r)

        for stage in range(LEVELS + 1):
            needs = t >= (reaches[stage - 1] if stage else 0)
            at(relay_at[stage], functools.partial(relay, stage), needs)
        for stage in range(1, LEVELS + 1):
            at(forward_at[stage], functools.partial(forward, stage), t >= reaches[stage - 1])
        for stage in range(LEVELS + 1):
            at(relay_at[stage] + 1, functools.partial(compute, stage), t >= 0)
        return carry

    lax.fori_loop(0, 3 * CHUNKS + 3, step, 0)

    def drain(r, carry):
        for stage in range(LEVELS + 1):
            @pl.when(t >= (reaches[stage - 1] if stage else 0))
            def _():
                to_partner(stage, r).wait_send()
                for k in range(1, halves):
                    to_other(stage, r, k).wait_send()
                    relayed(stage, r, k).wait_send()
        for stage in range(LEVELS):
            @pl.when(t + reaches[stage] < n_tm)
            def _():
                along(stage, r).wait_send()
        return carry

    lax.fori_loop(0, CHUNKS, drain, 0)


def body(transitions, start_weights):
    _, states, width = transitions.shape
    n_tm, n_panel = lax.axis_size("tm"), lax.axis_size("panel")
    others = n_panel // 2 - 1
    stages = LEVELS + 1
    dma = pltpu.SemaphoreType.DMA
    size = states * width * 4
    window, occupancy = pl.pallas_call(
        functools.partial(kernel, n_tm, n_panel),
        out_shape=(jax.ShapeDtypeStruct((states, width), jnp.float32),
                   jax.ShapeDtypeStruct((1, width), jnp.float32)),
        in_specs=[pl.BlockSpec(memory_space=pltpu.VMEM)] * 2,
        out_specs=[pl.BlockSpec(memory_space=pltpu.VMEM)] * 2,
        scratch_shapes=[
            pltpu.VMEM((stages, n_panel, states, width), jnp.float32),
            pltpu.VMEM((LEVELS, states, width), jnp.float32),
            pltpu.VMEM((stages, states, width), jnp.bfloat16),
            pltpu.VMEM((stages, states, width), jnp.bfloat16),
            dma((stages, CHUNKS)), dma((stages, CHUNKS)),
            dma((stages, others, CHUNKS)), dma((stages, others, CHUNKS)),
            dma((stages, others, CHUNKS)), dma((stages, others, CHUNKS)),
            dma((LEVELS, CHUNKS)), dma((LEVELS, CHUNKS)),
        ],
        compiler_params=pltpu.CompilerParams(
            collective_id=0, has_side_effects=True,
            vmem_limit_bytes=size * (stages * n_panel + 3 * stages + 8)),
    )(transitions, start_weights.reshape(CHUNKS, states // CHUNKS))
    window_kernel = window[None]
    return (window_kernel, occupancy)


def solution(mesh):
    placed = (P("tm", None, "panel"), P())
    return jax.shard_map(
        body,
        mesh=mesh,
        in_specs=placed,
        out_specs=(P("tm", None, "panel"), P("tm", "panel")),
        check_vma=False,
    )
```
